256 devices in a mesh: hid: 4 (over x), src: 32 (over z, y), tgt: 2 (over core).
Axes of the slice: x: 4, y: 4, z: 8, core: 2. Of those that a mesh axis runs over, the one named last changes fastest.
Arguments:
- decoder_slab: float32 [65536, 3584], P('src', 'hid'), may hold values from -1000 to 1000, as said below
- encoder_panel: float32 [3584, 1024], P(('hid', 'src'), 'tgt'), may hold values from -6 to 6
Outputs:
- virtual: float32 [65536, 2, 512], P('src', 'tgt', 'hid')
The draws below stay inside these ranges and needn't reach their ends.
Inputs may be any that keep to these rules, and one draw needn't show every extreme that they name: `decoder_slab`: float32 decoder rows.
All inputs are finite; a program needn't handle non-finite values.
Results may differ from the reference program's by a relative error of at most 0.000071.
Values sent between devices are 32-bit elements; how exact they have to be, the bound alone decides.
A program may use at most 128 MiB of HBM per device.

```python
import math
import jax
import jax.numpy as jnp
from jax import lax

H = 3584
TARGETS = 1024
SOURCES = 65536
PANELS = 2
SUB = 512


def draw_decoder_slab(key, part):
    key = jax.random.fold_in(key, 11)
    k_rows, k_cols, k_base = jax.random.split(key, 3)
    row_scale = jnp.exp(jax.random.uniform(k_rows, (SOURCES, 1), jnp.float32) * math.log(10.0))
    ramp = jnp.sqrt(1.0 + 2.0 * jnp.arange(H, dtype=jnp.float32) / H)
    col_scale = jnp.exp(jax.random.uniform(k_cols, (1, H), jnp.float32) * math.log(10.0)) * ramp[None, :]
    base = jnp.clip(jax.random.normal(k_base, (SOURCES, H), jnp.float32), -5.0, 5.0)
    return (base * row_scale * col_scale).astype(jnp.float32)


def steps_of(rng, shape, cuts, low, high):
    loudness = 1.0
    for dim, parts in cuts:
        draws = jax.random.uniform(jax.random.fold_in(jax.random.fold_in(rng, 6), dim), (parts,), jnp.float32, low / len(cuts), high / len(cuts))
        loudness = loudness * jnp.repeat(jnp.exp(draws), shape[dim] // parts).reshape((-1,) + (1,) * (len(shape) - 1 - dim))
    return loudness


def bell_draw(own_key, dims, spread, reach, cuts=(), kind=jnp.bfloat16):
    result = jax.random.normal(own_key, dims, jnp.float32) * spread
    if len(cuts) > 0:
        result = steps_of(own_key, dims, cuts, -0.22, 0.18) * result
    return jnp.clip(result, min=-reach, max=reach).astype(kind)


def setup_inputs(seed: int = 0) -> dict:
    seeds = jax.random.split(jax.random.key(seed), 3)
    return {
        "decoder_slab": draw_decoder_slab(jax.random.fold_in(seeds[2], 71), 0),
        "encoder_panel": bell_draw(seeds[1], (H, TARGETS), 1.0, 6.0, ((0, 128), (1, 2)), jnp.float32),
    }


def reference(decoder_slab, encoder_panel):
    block = min(SOURCES, 4096)
    pieces = decoder_slab.reshape(SOURCES // block, block, H)

    def one_block(rows):
        squares = lax.optimization_barrier(jnp.sum(rows * rows, axis=1, keepdims=True))
        inverse = lax.rsqrt(squares + 1e-06)
        unit_rows = rows * inverse
        return jnp.dot(unit_rows, encoder_panel, precision=lax.Precision.HIGHEST, preferred_element_type=jnp.float32)
    product = lax.map(one_block, pieces).reshape(SOURCES, TARGETS)
    return product.reshape(SOURCES, PANELS, SUB)
```

```python
import jax
import jax.numpy as jnp
from jax import lax
from jax.experimental import pallas as pl
from jax.experimental.pallas import tpu as pltpu
from jax.sharding import PartitionSpec as P

EPS = 1e-06
MESH = pl.DeviceIdType.MESH
NX, NY, NZ = 4, 4, 8
ROWS, K, W = 2048, 896, 128
HALF = ROWS // 2
SHARD = K // (NY * NZ)
DCH = 256
RB = 256
NB = HALF // RB
ZS = (4, 3, 5, 2, 6, 1, 7)
YS = (2, 1, 3)
XS = (2, 1, 3)
FAR, NEAR, SUM = 0, 1, 2
PLUS, MINUS = 0, 1


def kernel(d_ref, e_ref, o_ref, dbuf, ds, land, rhs, sq, sqin, out_x, in_x,
           dsem, esem, zss, zrs, yss, yrs, xss, xrs, qss, qrs):
    h = lax.axis_index("hid")
    s = lax.axis_index("src")
    z, y = s // NY, lax.rem(s, NY)

    def at_x(d):
        return {"hid": lax.rem(h + d, NX)}

    def at_z(d):
        return {"src": lax.rem(z + d, NZ) * NY + y}

    def at_y(d):
        return {"src": z * NY + lax.rem(y + d, NY)}

    def load(i):
        return pltpu.make_async_copy(
            d_ref.at[pl.ds(i * DCH, DCH)], dbuf.at[pl.ds(i * DCH, DCH)], dsem.at[i])

    def columns(u):
        t = lax.rem(h + u, NX)
        return e_ref.at[:, pl.ds(pl.multiple_of(t * W, W), W)]

    def own_piece(u):
        return pltpu.make_async_copy(columns(u), land.at[u, z, y], esem.at[u])

    def z_send(u, i):
        return pltpu.make_async_remote_copy(
            src_ref=columns(u), dst_ref=land.at[u, z, y], send_sem=zss.at[u, i], recv_sem=zrs.at[u, i],
            device_id=at_z(ZS[i]), device_id_type=MESH)

    def y_send(u, i, j):
        zz = z if i == NZ - 1 else lax.rem(z + NZ - ZS[i], NZ)
        return pltpu.make_async_remote_copy(
            src_ref=land.at[u, zz, y], dst_ref=land.at[u, zz, y], send_sem=yss.at[u, i, j],
            recv_sem=yrs.at[u, i, j], device_id=at_y(YS[j]), device_id_type=MESH)

    def sq_send(i):
        return pltpu.make_async_remote_copy(
            src_ref=sq, dst_ref=sqin.at[i], send_sem=qss.at[i], recv_sem=qrs.at[i],
            device_id=at_x(XS[i]), device_id_type=MESH)

    def x_send(part, way, b):
        return pltpu.make_async_remote_copy(
            src_ref=out_x.at[part, way, pl.ds(b * RB, RB)], dst_ref=in_x.at[part, way, pl.ds(b * RB, RB)],
            send_sem=xss.at[part, way, b], recv_sem=xrs.at[part, way, b],
            device_id=at_x(1 if way == PLUS else 3), device_id_type=MESH)

    def split(i):
        load(i).wait()
        d = dbuf[pl.ds(i * DCH, DCH), :]
        hi = d.astype(jnp.bfloat16)
        ds[pl.ds(i * DCH, DCH), 0:K] = hi
        ds[pl.ds(i * DCH, DCH), K:2 * K] = (d - hi.astype(jnp.float32)).astype(jnp.bfloat16)
        p = d[:, 0:W] * d[:, 0:W]
        for c in range(1, K // W):
            q = d[:, c * W:(c + 1) * W]
            p = p + q * q
        for c in range(DCH // W):
            row = jnp.sum(p[c * W:(c + 1) * W].T, axis=0, keepdims=True)
            sq[i * (DCH // W) + c:i * (DCH // W) + c + 1, :] = row

    def z_start(u):
        for i in range(NZ - 1):
            z_send(u, i).start()

    def y_start(u):
        own_piece(u).wait()
        for j in range(3):
            y_send(u, NZ - 1, j).start()
        for i in range(NZ - 1):
            z_send(u, i).wait_recv()
            for j in range(3):
                y_send(u, i, j).start()

    def y_wait(u):
        for i in range(NZ):
            for j in range(3):
                y_send(u, i, j).wait_recv()

    def panel(u):
        for a in range(NZ):
            for b in range(0, NY, 4):
                e = jnp.concatenate([land[u, a, b + k] for k in range(4)], axis=0)
                hi = e.astype(jnp.bfloat16)
                lo = (e - hi.astype(jnp.float32)).astype(jnp.bfloat16)
                r = (a * NY + b) * SHARD
                for off in (0, K):
                    rhs[u, off + r:off + r + 4 * SHARD, 0:W] = hi
                    rhs[u, off + r:off + r + 4 * SHARD, W:2 * W] = lo

    def product(u, r):
        full = jnp.dot(ds[pl.ds(r, RB), :], rhs[u], preferred_element_type=jnp.float32)
        return full[:, 0:W] + full[:, W:2 * W]

    for i in range(ROWS // DCH):
        load(i).start()
    for u in (2, 1, 3, 0):
        own_piece(u).start()
    barrier = pltpu.get_barrier_semaphore()
    for peer in [at_z(d) for d in ZS] + [at_y(d) for d in YS] + [at_x(d) for d in XS]:
        pl.semaphore_signal(barrier, inc=1, device_id=peer, device_id_type=MESH)
    pl.semaphore_wait(barrier, len(ZS) + len(YS) + len(XS))

    z_start(2)
    for i in range(0, 4):
        split(i)
    y_start(2)
    z_start(1)
    z_start(3)
    for i in range(4, 8):
        split(i)
    for i in range(3):
        sq_send(i).start()
    y_wait(2)
    panel(2)

    def far_block(b):
        for way, base in ((PLUS, HALF), (MINUS, 0)):
            out_x[FAR, way, pl.ds(b * RB, RB), :] = product(2, base + b * RB)
            x_send(FAR, way, b).start()

    for b in range(0, NB // 2):
        far_block(b)
    y_start(1)
    y_start(3)
    for b in range(NB // 2, NB):
        far_block(b)
    z_start(0)
    y_wait(1)
    panel(1)
    y_wait(3)
    panel(3)
    for b in range(NB):
        for way, base, u in ((PLUS, 0, 1), (MINUS, HALF, 3)):
            out_x[NEAR, way, pl.ds(b * RB, RB), :] = product(u, base + b * RB)
            x_send(NEAR, way, b).start()
    y_start(0)
    for b in range(NB):
        for way, base, u in ((PLUS, HALF, 1), (MINUS, 0, 3)):
            mine = product(u, base + b * RB)
            x_send(FAR, way, b).wait_recv()
            out_x[SUM, way, pl.ds(b * RB, RB), :] = mine + in_x[FAR, way, pl.ds(b * RB, RB), :]
            x_send(SUM, way, b).start()
    y_wait(0)
    panel(0)
    for b in range(ROWS // RB):
        o_ref[pl.ds(b * RB, RB), :] = product(0, b * RB)
    for i in range(3):
        sq_send(i).wait_recv()
    inverse = lax.rsqrt(sq[...] + sqin[0] + sqin[1] + sqin[2] + EPS)
    for b in range(NB):
        x_send(NEAR, PLUS, b).wait_recv()
        x_send(NEAR, MINUS, b).wait_recv()
        for way, base, near in ((PLUS, HALF, MINUS), (MINUS, 0, PLUS)):
            x_send(SUM, way, b).wait_recv()
            r = base + b * RB
            total = (o_ref[pl.ds(r, RB), :] + in_x[NEAR, near, pl.ds(b * RB, RB), :]
                     + in_x[SUM, way, pl.ds(b * RB, RB), :])
            for c in range(RB // W):
                i = r // W + c
                scale = jnp.broadcast_to(inverse[i:i + 1, :], (W, W)).T
                o_ref[pl.ds(r + c * W, W), :] = total[c * W:(c + 1) * W] * scale

    for u in range(NX):
        for i in range(NZ - 1):
            z_send(u, i).wait_send()
        for i in range(NZ):
            for j in range(3):
                y_send(u, i, j).wait_send()
    for i in range(3):
        sq_send(i).wait_send()
    for part in range(3):
        for way in range(2):
            for b in range(NB):
                x_send(part, way, b).wait_send()


def shards(decoder_slab, encoder_panel):
    f32, bf16 = jnp.float32, jnp.bfloat16
    dma = pltpu.SemaphoreType.DMA
    out = pl.pallas_call(
        kernel,
        out_shape=jax.ShapeDtypeStruct((ROWS, W), f32),
        in_specs=[pl.BlockSpec(memory_space=pl.ANY)] * 2,
        out_specs=pl.BlockSpec(memory_space=pltpu.VMEM),
        scratch_shapes=[
            pltpu.VMEM((ROWS, K), f32),
            pltpu.VMEM((ROWS, 2 * K), bf16),
            pltpu.VMEM((NX, NZ, NY, SHARD, W), f32),
            pltpu.VMEM((NX, 2 * K, 2 * W), bf16),
            pltpu.VMEM((ROWS // W, W), f32),
            pltpu.VMEM((3, ROWS // W, W), f32),
            pltpu.VMEM((3, 2, HALF, W), f32),
            pltpu.VMEM((3, 2, HALF, W), f32),
            dma((ROWS // DCH,)), dma((NX,)),
            dma((NX, NZ - 1)), dma((NX, NZ - 1)),
            dma((NX, NZ, 3)), dma((NX, NZ, 3)),
            dma((3, 2, NB)), dma((3, 2, NB)),
            dma((3,)), dma((3,)),
        ],
        compiler_params=pltpu.CompilerParams(
            collective_id=0, has_side_effects=True, vmem_limit_bytes=56 * 1024 * 1024),
    )(decoder_slab, encoder_panel)
    return out.reshape(ROWS, 1, W)


def solution(mesh):
    placed = (P("src", "hid"), P(("hid", "src"), "tgt"))
    return jax.shard_map(
        shards, mesh=mesh, in_specs=placed, out_specs=P("src", "tgt", "hid"), check_vma=False
    )
```

```python
import jax
import jax.numpy as jnp
from jax import lax
from jax.experimental import pallas as pl
from jax.experimental.pallas import tpu as pltpu
from jax.sharding import PartitionSpec as P

EPS = 1e-06
MESH = pl.DeviceIdType.MESH
NX, NY, NZ = 4, 4, 8
ROWS, K, W = 2048, 896, 128
HALF = ROWS // 2
SHARD = K // (NY * NZ)
DCH = 256
RB = 256
NB = HALF // RB
ZS = (4, 3, 5, 2, 6, 1, 7)
YS = (2, 1, 3)
XS = (2, 1, 3)
FAR, NEAR, SUM = 0, 1, 2
PLUS, MINUS = 0, 1


def kernel(d_ref, e_ref, o_ref, dbuf, ds, land, rhs, sq, sqin, out_x, in_x,
           dsem, esem, zss, zrs, yss, yrs, xss, xrs, qss, qrs):
    h = lax.axis_index("hid")
    s = lax.axis_index("src")
    z, y = s // NY, lax.rem(s, NY)

    def at_x(d):
        return {"hid": lax.rem(h + d, NX)}

    def at_z(d):
        return {"src": lax.rem(z + d, NZ) * NY + y}

    def at_y(d):
        return {"src": z * NY + lax.rem(y + d, NY)}

    def load(i):
        return pltpu.make_async_copy(
            d_ref.at[pl.ds(i * DCH, DCH)], dbuf.at[pl.ds(i * DCH, DCH)], dsem.at[i])

    def columns(u):
        t = lax.rem(h + u, NX)
        return e_ref.at[:, pl.ds(pl.multiple_of(t * W, W), W)]

    def own_piece(u):
        return pltpu.make_async_copy(columns(u), land.at[u, z, y], esem.at[u])

    def z_send(u, i):
        return pltpu.make_async_remote_copy(
            src_ref=columns(u), dst_ref=land.at[u, z, y], send_sem=zss.at[u, i], recv_sem=zrs.at[u, i],
            device_id=at_z(ZS[i]), device_id_type=MESH)

    def y_send(u, i, j):
        zz = z if i == NZ - 1 else lax.rem(z + NZ - ZS[i], NZ)
        return pltpu.make_async_remote_copy(
            src_ref=land.at[u, zz, y], dst_ref=land.at[u, zz, y], send_sem=yss.at[u, i, j],
            recv_sem=yrs.at[u, i, j], device_id=at_y(YS[j]), device_id_type=MESH)

    def sq_send(i):
        return pltpu.make_async_remote_copy(
            src_ref=sq, dst_ref=sqin.at[i], send_sem=qss.at[i], recv_sem=qrs.at[i],
            device_id=at_x(XS[i]), device_id_type=MESH)

    def x_send(part, way, b):
        return pltpu.make_async_remote_copy(
            src_ref=out_x.at[part, way, pl.ds(b * RB, RB)], dst_ref=in_x.at[part, way, pl.ds(b * RB, RB)],
            send_sem=xss.at[part, way, b], recv_sem=xrs.at[part, way, b],
            device_id=at_x(1 if way == PLUS else 3), device_id_type=MESH)

    def split(i):
        load(i).wait()
        d = dbuf[pl.ds(i * DCH, DCH), :]
        hi = d.astype(jnp.bfloat16)
        ds[pl.ds(i * DCH, DCH), 0:K] = hi
        ds[pl.ds(i * DCH, DCH), K:2 * K] = (d - hi.astype(jnp.float32)).astype(jnp.bfloat16)
        p = d[:, 0:W] * d[:, 0:W]
        for c in range(1, K // W):
            q = d[:, c * W:(c + 1) * W]
            p = p + q * q
        for c in range(DCH // W):
            row = jnp.sum(p[c * W:(c + 1) * W].T, axis=0, keepdims=True)
            sq[i * (DCH // W) + c:i * (DCH // W) + c + 1, :] = row

    sent, due = [], {}

    def go(make, *key):
        copy = make(*key)
        copy.start()
        sent.append(copy)
        due[(make,) + key] = copy

    def got(make, *key):
        due.pop((make,) + key).wait_recv()

    def z_start(u):
        for i in range(NZ - 1):
            go(z_send, u, i)

    def y_start(u):
        own_piece(u).wait()
        for j in range(3):
            go(y_send, u, NZ - 1, j)
        for i in range(NZ - 1):
            got(z_send, u, i)
            for j in range(3):
                go(y_send, u, i, j)

    def y_wait(u):
        for i in range(NZ):
            for j in range(3):
                got(y_send, u, i, j)

    def panel(u):
        for a in range(NZ):
            e = jnp.concatenate([land[u, a, k] for k in range(NY)], axis=0)
            hi = e.astype(jnp.bfloat16)
            lo = (e - hi.astype(jnp.float32)).astype(jnp.bfloat16)
            r = a * NY * SHARD
            for off in (0, K):
                rhs[u, off + r:off + r + NY * SHARD, 0:W] = hi
                rhs[u, off + r:off + r + NY * SHARD, W:2 * W] = lo

    def product(u, r, n=RB):
        full = jnp.dot(ds[pl.ds(r, n), :], rhs[u], preferred_element_type=jnp.float32)
        return full[:, 0:W] + full[:, W:2 * W]

    def finish():
        for copy in due.values():
            copy.wait_recv()
        for copy in sent:
            copy.wait_send()

    barrier = pltpu.get_barrier_semaphore()
    for peer in [at_z(d) for d in ZS] + [at_y(d) for d in YS] + [at_x(d) for d in XS]:
        pl.semaphore_signal(barrier, inc=1, device_id=peer, device_id_type=MESH)
    own_piece(2).start()
    pl.semaphore_wait(barrier, len(ZS) + len(YS) + len(XS))
    z_start(2)
    for i in range(ROWS // DCH):
        load(i).start()
    for u in (1, 3, 0):
        own_piece(u).start()
    z_start(1)
    z_start(3)
    for i in range(0, 4):
        split(i)
    y_start(2)
    for i in range(4, 8):
        split(i)
    for i in range(3):
        go(sq_send, i)
    y_wait(2)
    panel(2)

    def far_block(b):
        for way, base in ((PLUS, HALF), (MINUS, 0)):
            out_x[FAR, way, pl.ds(b * RB, RB), :] = product(2, base + b * RB)
            go(x_send, FAR, way, b)

    for b in range(0, NB // 2):
        far_block(b)
    y_start(1)
    y_start(3)
    for b in range(NB // 2, NB):
        far_block(b)
    z_start(0)
    y_wait(1)
    panel(1)
    y_wait(3)
    panel(3)
    for b in range(NB):
        for way, base, u in ((PLUS, 0, 1), (MINUS, HALF, 3)):
            out_x[NEAR, way, pl.ds(b * RB, RB), :] = product(u, base + b * RB)
            go(x_send, NEAR, way, b)
    y_start(0)
    for b in range(NB):
        for way, base, u in ((PLUS, HALF, 1), (MINUS, 0, 3)):
            mine = product(u, base + b * RB)
            got(x_send, FAR, way, b)
            out_x[SUM, way, pl.ds(b * RB, RB), :] = mine + in_x[FAR, way, pl.ds(b * RB, RB), :]
            go(x_send, SUM, way, b)
    y_wait(0)
    panel(0)
    for b in range(ROWS // RB):
        o_ref[pl.ds(b * RB, RB), :] = product(0, b * RB)
    for i in range(3):
        got(sq_send, i)
    inverse = lax.rsqrt(sq[...] + sqin[0] + sqin[1] + sqin[2] + EPS)
    for b in range(NB):
        got(x_send, NEAR, PLUS, b)
        got(x_send, NEAR, MINUS, b)
        for way, base, near in ((PLUS, HALF, MINUS), (MINUS, 0, PLUS)):
            got(x_send, SUM, way, b)
            r = base + b * RB
            total = (o_ref[pl.ds(r, RB), :] + in_x[NEAR, near, pl.ds(b * RB, RB), :]
                     + in_x[SUM, way, pl.ds(b * RB, RB), :])
            for c in range(RB // W):
                i = r // W + c
                scale = jnp.broadcast_to(inverse[i:i + 1, :], (W, W)).T
                o_ref[pl.ds(r + c * W, W), :] = total[c * W:(c + 1) * W] * scale
    finish()


def shards(decoder_slab, encoder_panel):
    f32, bf16 = jnp.float32, jnp.bfloat16
    dma = pltpu.SemaphoreType.DMA
    out = pl.pallas_call(
        kernel,
        out_shape=pltpu.VMEM((ROWS, W), f32),
        in_specs=[pl.BlockSpec(memory_space=pl.ANY)] * 2,
        out_specs=pl.BlockSpec(memory_space=pltpu.VMEM),
        scratch_shapes=[
            pltpu.VMEM((ROWS, K), f32),
            pltpu.VMEM((ROWS, 2 * K), bf16),
            pltpu.VMEM((NX, NZ, NY, SHARD, W), f32),
            pltpu.VMEM((NX, 2 * K, 2 * W), bf16),
            pltpu.VMEM((ROWS // W, W), f32),
            pltpu.VMEM((3, ROWS // W, W), f32),
            pltpu.VMEM((3, 2, HALF, W), f32),
            pltpu.VMEM((3, 2, HALF, W), f32),
            dma((ROWS // DCH,)), dma((NX,)),
            dma((NX, NZ - 1)), dma((NX, NZ - 1)),
            dma((NX, NZ, 3)), dma((NX, NZ, 3)),
            dma((3, 2, NB)), dma((3, 2, NB)),
            dma((3,)), dma((3,)),
        ],
        compiler_params=pltpu.CompilerParams(
            collective_id=0, has_side_effects=True, vmem_limit_bytes=56 * 1024 * 1024),
    )(decoder_slab, encoder_panel)
    return out.reshape(ROWS, 1, W)


def solution(mesh):
    placed = (P("src", "hid"), P(("hid", "src"), "tgt"))
    return jax.shard_map(
        shards, mesh=mesh, in_specs=placed, out_specs=P("src", "tgt", "hid"), check_vma=False
    )
```

```python
import jax
import jax.numpy as jnp
from jax import lax
from jax.experimental import pallas as pl
from jax.experimental.pallas import tpu as pltpu
from jax.sharding import PartitionSpec as P

EPS = 1e-06
MESH = pl.DeviceIdType.MESH
NX, NY, NZ = 4, 4, 8
ROWS, K, W = 2048, 896, 128
SHARD = K // (NY * NZ)
CARRY = 160
PIECE = CARRY // 4
KEPT = ROWS - CARRY
HALF = KEPT // 2
BLOCKS = ((0, 240), (240, 240), (480, 240), (720, 224))
NB = len(BLOCKS)
DCH = 256
ZS = (4, 3, 5, 2, 6, 1, 7)
YS = (2, 1, 3)
XS = (2, 1, 3)
UNIT = (2, 1, 3, 0)
GROUPS = ((0, 1), (1, 2), (3, 1), (4, 3))
FAR, NEAR, SUM = 0, 1, 2
PLUS, MINUS = 0, 1


def kernel(d_ref, e_ref, o_ref, dbuf, ds, land, rhs, sq, sqin, scale, out_x, in_x, car, cds,
           dsem, esem, pss, prs, zss, zrs, yss, yrs, wss, wrs, fss, frs, xss, xrs, qss, qrs, css, crs):
    h = lax.axis_index("hid")
    s = lax.axis_index("src")
    core = lax.axis_index("tgt")
    z, y = s // NY, lax.rem(s, NY)

    def at_x(d):
        return {"hid": lax.rem(h + d, NX)}

    def at_z(d):
        return {"src": lax.rem(z + d, NZ) * NY + y}

    def at_y(d):
        return {"src": z * NY + lax.rem(y + d, NY)}

    def remote(src, dst, send, recv, peer):
        return pltpu.make_async_remote_copy(
            src_ref=src, dst_ref=dst, send_sem=send, recv_sem=recv, device_id=peer, device_id_type=MESH)

    def load(i):
        return pltpu.make_async_copy(
            d_ref.at[pl.ds(i * DCH, DCH)], dbuf.at[pl.ds(i * DCH, DCH)], dsem.at[i])

    def columns(d):
        t = lax.rem(h + d, NX)
        return e_ref.at[:, pl.ds(pl.multiple_of(t * W, W), W)]

    def own_piece(u):
        return pltpu.make_async_copy(columns(UNIT[u]), land.at[u, z, y], esem.at[u])

    def piece_send(d):
        return remote(columns(d), land.at[7 - d, z, y], pss.at[d - 1], prs.at[d - 1], at_x(d))

    def z_send(g, i):
        if g == 0:
            src, dst = columns(UNIT[0]), land.at[0, z, y]
        else:
            src = dst = land.at[pl.ds(*GROUPS[g]), z, y]
        return remote(src, dst, zss.at[g, i], zrs.at[g, i], at_z(ZS[i]))

    def first_send(i, j):
        zz = z if i == NZ - 1 else lax.rem(z + NZ - ZS[i], NZ)
        return remote(land.at[0, zz, y], land.at[0, zz, y], yss.at[i, j], yrs.at[i, j], at_y(YS[j]))

    def column_send(g, way):
        part = land.at[pl.ds(*GROUPS[g]), :, y]
        return remote(part, part, wss.at[g, way], wrs.at[g, way], at_y(1 if way == PLUS else 3))

    def half_send(g, way):
        yy = lax.rem(y + (3 if way == PLUS else 1), NY)
        part = land.at[pl.ds(*GROUPS[g]), pl.ds(0 if way == PLUS else NZ // 2, NZ // 2), yy]
        return remote(part, part, fss.at[g, way], frs.at[g, way], at_y(1 if way == PLUS else 3))

    def sq_send(i):
        return remote(sq, sqin.at[i], qss.at[i], qrs.at[i], at_x(XS[i]))

    def x_send(part, way, b):
        rows = pl.ds(*BLOCKS[b])
        return remote(out_x.at[part, way, rows], in_x.at[part, way, rows], xss.at[part, way, b],
                      xrs.at[part, way, b], at_x(1 if way == PLUS else 3))

    def carry_send(way, p):
        r = pl.multiple_of(KEPT + core * (2 * PIECE) + p * PIECE, 8)
        return remote(d_ref.at[pl.ds(r, PIECE)], car.at[core, 2 if way == PLUS else 0, p],
                      css.at[way, p], crs.at[way, p], at_x(1 if way == PLUS else 3))

    def carry_on(way):
        p = 0 if way == PLUS else 1
        return remote(car.at[core, 2 if way == PLUS else 0, p], car.at[core, 1, p],
                      css.at[way, 2], crs.at[way, 2], at_x(1 if way == PLUS else 3))

    def carry_share():
        return remote(car.at[core], car.at[core], css.at[2, 0], crs.at[2, 0], {"tgt": 1 - core})

    def halves(d):
        hi = d.astype(jnp.bfloat16)
        return hi, (d - hi.astype(jnp.float32)).astype(jnp.bfloat16)

    def split(i):
        load(i).wait()
        d = dbuf[pl.ds(i * DCH, DCH), :]
        hi, lo = halves(d)
        ds[pl.ds(i * DCH, DCH), 0:K] = hi
        ds[pl.ds(i * DCH, DCH), K:2 * K] = lo
        p = d[:, 0:W] * d[:, 0:W]
        for c in range(1, K // W):
            q = d[:, c * W:(c + 1) * W]
            p = p + q * q
        for c in range(DCH // W):
            row = jnp.sum(p[c * W:(c + 1) * W].T, axis=0, keepdims=True)
            sq[i * (DCH // W) + c:i * (DCH // W) + c + 1, :] = row

    sent, due = [], {}

    def go(make, *key):
        copy = make(*key)
        copy.start()
        sent.append(copy)
        due[(make,) + key] = copy

    def got(make, *key):
        due.pop((make,) + key).wait_recv()

    def z_start(g):
        for i in range(NZ - 1):
            go(z_send, g, i)

    def z_wait(g):
        for i in range(NZ - 1):
            got(z_send, g, i)

    def columns_start(g):
        z_wait(g)
        for way in (PLUS, MINUS):
            go(column_send, g, way)

    def halves_start(g):
        for way in (PLUS, MINUS):
            got(column_send, g, way)
            go(half_send, g, way)

    def halves_wait(g):
        for way in (PLUS, MINUS):
            got(half_send, g, way)

    def panel(u):
        for a in range(NZ):
            e = jnp.concatenate([land[u, a, k] for k in range(NY)], axis=0)
            hi, lo = halves(e)
            r = a * NY * SHARD
            for off in (0, K):
                rhs[u, off + r:off + r + NY * SHARD, 0:W] = hi
                rhs[u, off + r:off + r + NY * SHARD, W:2 * W] = lo

    def dot(left, u):
        full = jnp.dot(left, rhs[u], preferred_element_type=jnp.float32)
        return full[:, 0:W] + full[:, W:2 * W]

    def product(u, r, n):
        return dot(ds[pl.ds(r, n), :], u)

    barrier = pltpu.get_barrier_semaphore()
    peers = [at_z(d) for d in ZS] + [at_y(d) for d in YS] + [at_x(d) for d in XS] + [{"tgt": 1 - core}]
    for peer in peers:
        pl.semaphore_signal(barrier, inc=1, device_id=peer, device_id_type=MESH)
    for u in range(NX):
        own_piece(u).start()
    pl.semaphore_wait(barrier, len(peers))

    z_start(0)
    for d in XS:
        go(piece_send, d)
    for p in (0, 1):
        go(carry_send, PLUS, p)
        go(carry_send, MINUS, 1 - p)
    for i in range(ROWS // DCH):
        load(i).start()
    for u in range(NX):
        own_piece(u).wait()
    z_start(1)
    for i in range(0, 4):
        split(i)
    for j in range(3):
        go(first_send, NZ - 1, j)
    for i in range(NZ - 1):
        got(z_send, 0, i)
        for j in range(3):
            go(first_send, i, j)
    got(carry_send, PLUS, 0)
    go(carry_on, PLUS)
    got(carry_send, MINUS, 1)
    go(carry_on, MINUS)
    for i in range(4, 8):
        split(i)
    for i in range(3):
        go(sq_send, i)
    for d in XS:
        got(piece_send, d)
    z_start(2)
    z_start(3)
    columns_start(1)
    for i in range(NZ):
        for j in range(3):
            got(first_send, i, j)
    panel(0)

    for b, (r, n) in enumerate(BLOCKS):
        for way, base in ((PLUS, HALF), (MINUS, 0)):
            out_x[FAR, way, pl.ds(r, n), :] = product(0, base + r, n)
            go(x_send, FAR, way, b)
    halves_start(1)
    columns_start(2)
    columns_start(3)
    halves_wait(1)
    panel(1)
    panel(2)
    for b, (r, n) in enumerate(BLOCKS):
        for way, base, u in ((PLUS, 0, 1), (MINUS, HALF, 2)):
            out_x[NEAR, way, pl.ds(r, n), :] = product(u, base + r, n)
            go(x_send, NEAR, way, b)
    for b, (r, n) in enumerate(BLOCKS):
        for way, base, u in ((PLUS, HALF, 1), (MINUS, 0, 2)):
            mine = product(u, base + r, n)
            got(x_send, FAR, way, b)
            out_x[SUM, way, pl.ds(r, n), :] = mine + in_x[FAR, way, pl.ds(r, n), :]
            go(x_send, SUM, way, b)

    got(carry_send, PLUS, 1)
    got(carry_send, MINUS, 0)
    got(carry_on, PLUS)
    got(carry_on, MINUS)
    go(carry_share)
    halves_start(2)
    halves_start(3)
    for i in range(3):
        got(sq_send, i)
    inverse = lax.rsqrt(sq[...] + sqin[0] + sqin[1] + sqin[2] + EPS)
    for i in range(ROWS // W):
        scale[i * W:(i + 1) * W, :] = jnp.broadcast_to(inverse[i:i + 1, :], (W, W)).T
    got(carry_share)
    for k in range(3):
        for c in range(2):
            d = jnp.concatenate([car[c, k, 0], car[c, k, 1]], axis=0)
            hi, lo = halves(d)
            cds[k, c * 2 * PIECE:(c + 1) * 2 * PIECE, 0:K] = hi
            cds[k, c * 2 * PIECE:(c + 1) * 2 * PIECE, K:2 * K] = lo
    halves_wait(2)
    panel(3)
    for r, n in [(r, 256) for r in range(0, ROWS, 256)]:
        o_ref[pl.ds(r, n), :] = product(3, r, n)
    halves_wait(3)
    for u in (4, 5, 6):
        panel(u)
    total = o_ref[KEPT:ROWS, :]
    for k in range(3):
        total = total + dot(cds[k], 4 + k)
    o_ref[KEPT:ROWS, :] = total * scale[KEPT:ROWS, :]

    for b, (r, n) in enumerate(BLOCKS):
        got(x_send, NEAR, PLUS, b)
        got(x_send, NEAR, MINUS, b)
        for way, base, near in ((PLUS, HALF, MINUS), (MINUS, 0, PLUS)):
            got(x_send, SUM, way, b)
            rows = pl.ds(base + r, n)
            o_ref[rows, :] = (o_ref[rows, :] + in_x[NEAR, near, pl.ds(r, n), :]
                              + in_x[SUM, way, pl.ds(r, n), :]) * scale[rows, :]

    for copy in due.values():
        copy.wait_recv()
    for copy in sent:
        copy.wait_send()


def shards(decoder_slab, encoder_panel):
    f32, bf16 = jnp.float32, jnp.bfloat16
    dma = pltpu.SemaphoreType.DMA
    ng = len(GROUPS)
    out = pl.pallas_call(
        kernel,
        out_shape=pltpu.VMEM((ROWS, W), f32),
        in_specs=[pl.BlockSpec(memory_space=pl.ANY)] * 2,
        out_specs=pl.BlockSpec(memory_space=pltpu.VMEM),
        scratch_shapes=[
            pltpu.VMEM((ROWS, K), f32),
            pltpu.VMEM((ROWS, 2 * K), bf16),
            pltpu.VMEM((7, NZ, NY, SHARD, W), f32),
            pltpu.VMEM((7, 2 * K, 2 * W), bf16),
            pltpu.VMEM((ROWS // W, W), f32),
            pltpu.VMEM((3, ROWS // W, W), f32),
            pltpu.VMEM((ROWS, W), f32),
            pltpu.VMEM((3, 2, HALF, W), f32),
            pltpu.VMEM((3, 2, HALF, W), f32),
            pltpu.VMEM((2, 3, 2, PIECE, K), f32),
            pltpu.VMEM((3, CARRY, 2 * K), bf16),
            dma((ROWS // DCH,)), dma((NX,)),
            dma((3,)), dma((3,)),
            dma((ng, NZ - 1)), dma((ng, NZ - 1)),
            dma((NZ, 3)), dma((NZ, 3)),
            dma((ng, 2)), dma((ng, 2)),
            dma((ng, 2)), dma((ng, 2)),
            dma((3, 2, NB)), dma((3, 2, NB)),
            dma((3,)), dma((3,)),
            dma((3, 3)), dma((3, 3)),
        ],
        compiler_params=pltpu.CompilerParams(
            collective_id=0, has_side_effects=True, vmem_limit_bytes=56 * 1024 * 1024),
    )(decoder_slab, encoder_panel)
    return out.reshape(ROWS, 1, W)


def solution(mesh):
    placed = (P("src", "hid"), P(("hid", "src"), "tgt"))
    return jax.shard_map(
        shards, mesh=mesh, in_specs=placed, out_specs=P("src", "tgt", "hid"), check_vma=False
    )
```

```python
import jax
import jax.numpy as jnp
from jax import lax
from jax.experimental import pallas as pl
from jax.experimental.pallas import tpu as pltpu
from jax.sharding import PartitionSpec as P

EPS = 1e-06
MESH = pl.DeviceIdType.MESH
NX, NY, NZ = 4, 4, 8
ROWS, K, W = 2048, 896, 128
SHARD = K // (NY * NZ)
PAIR = 256
PART = PAIR // 2
KEPT = ROWS - 2 * PAIR
HALF = KEPT // 2
BLOCKS = ((0, 128), (128, 256), (384, 256), (640, 128))
NB = len(BLOCKS)
DCH = 256
ZS = (1, 7, 2, 6, 3, 5, 4)
YS = (2, 1, 3)
XS = (2, 1, 3)
OWN = {0: 2, 1: 1, 2: 3, 5: 0}
PIECES = ((4, 2, 1), (3, 2, 3), (7, 1, 1), (6, 3, 3))
GROUPS = ((0, 1), (1, 1), (2, 1), (3, 2), (5, 2), (7, 1))
Y_FIRST = (2, 5)
FAR, NEAR, SUM = 0, 1, 2
PLUS, MINUS = 0, 1


def kernel(d_ref, e_ref, o_ref, dbuf, ds, land, rhs, sq, sqin, scale, out_x, in_x, out_p, in_p, car, cds,
           dsem, esem, pss, prs, zss, zrs, yss, yrs, uss, urs, vss, vrs, wss, wrs, fss, frs, xss, xrs, qss, qrs, css, crs, ass, ars):
    h = lax.axis_index("hid")
    s = lax.axis_index("src")
    core = lax.axis_index("tgt")
    z, y = s // NY, lax.rem(s, NY)
    odd = lax.rem(h, 2)
    pairs = (KEPT + odd * PAIR, KEPT + (1 - odd) * PAIR)

    def at_x(d):
        return {"hid": lax.rem(h + d, NX)}

    def at_z(d):
        return {"src": lax.rem(z + d, NZ) * NY + y}

    def at_y(d):
        return {"src": z * NY + lax.rem(y + d, NY)}

    def remote(src, dst, send, recv, peer):
        return pltpu.make_async_remote_copy(
            src_ref=src, dst_ref=dst, send_sem=send, recv_sem=recv, device_id=peer, device_id_type=MESH)

    def load(i):
        return pltpu.make_async_copy(
            d_ref.at[pl.ds(i * DCH, DCH)], dbuf.at[pl.ds(i * DCH, DCH)], dsem.at[i])

    def columns(d):
        t = lax.rem(h + d, NX)
        return e_ref.at[:, pl.ds(pl.multiple_of(t * W, W), W)]

    def own_piece(u):
        return pltpu.make_async_copy(columns(OWN[u]), land.at[u, z, y], esem.at[u])

    def piece_send(i):
        unit, d, peer = PIECES[i]
        return remote(columns(d), land.at[unit, z, y], pss.at[i], prs.at[i], at_x(peer))

    def z_send(i):
        return remote(columns(OWN[0]), land.at[0, z, y], zss.at[i], zrs.at[i], at_z(ZS[i]))

    def bundle(g, zz):
        return land.at[pl.ds(*GROUPS[g]), zz] if g in Y_FIRST else land.at[pl.ds(*GROUPS[g]), zz, y]

    def near_send(g, i):
        part = bundle(g, z)
        return remote(part, part, uss.at[g, i], urs.at[g, i], at_z((2, 6, 1, 7)[i]))

    def on_send(g, i):
        came, to = ((6, 1), (2, 7), (6 + 4 * core, 2 + 4 * core))[i]
        part = bundle(g, lax.rem(z + came, NZ))
        return remote(part, part, vss.at[g, i], vrs.at[g, i], at_z(to))

    def row_send(g, j):
        part = land.at[pl.ds(*GROUPS[g]), z, y]
        return remote(part, part, wss.at[g, j], wrs.at[g, j], at_y(YS[j]))

    def first_send(i, j):
        zz = z if i == NZ - 1 else lax.rem(z + NZ - ZS[i], NZ)
        return remote(land.at[0, zz, y], land.at[0, zz, y], yss.at[i, j], yrs.at[i, j], at_y(YS[j]))

    def column_send(g, way):
        part = land.at[pl.ds(*GROUPS[g]), :, y]
        return remote(part, part, wss.at[g, way], wrs.at[g, way], at_y(1 if way == PLUS else 3))

    def half_send(g, way):
        yy = lax.rem(y + (3 if way == PLUS else 1), NY)
        part = land.at[pl.ds(*GROUPS[g]), pl.ds(0 if way == PLUS else NZ // 2, NZ // 2), yy]
        return remote(part, part, fss.at[g, way], frs.at[g, way], at_y(1 if way == PLUS else 3))

    def sq_send(i):
        return remote(sq, sqin.at[i], qss.at[i], qrs.at[i], at_x(XS[i]))

    def x_send(part, way, b):
        rows = pl.ds(*BLOCKS[b])
        return remote(out_x.at[part, way, rows], in_x.at[part, way, rows], xss.at[part, way, b],
                      xrs.at[part, way, b], at_x(1 if way == PLUS else 3))

    def pair_send(way):
        r = pl.multiple_of(pairs[way] + core * PART, 16)
        return remote(d_ref.at[pl.ds(r, PART)], car.at[core, 1 - way], css.at[way], crs.at[way],
                      at_x(1 if way == PLUS else 3))

    def pair_share():
        return remote(car.at[core], car.at[core], css.at[2], crs.at[2], {"tgt": 1 - core})

    def pair_sum_send(way):
        return remote(out_p.at[way], in_p.at[way], ass.at[way], ars.at[way], at_x(1 if way == PLUS else 3))

    def pair_rows(which):
        return pl.ds(pl.multiple_of(pairs[which], 16), PAIR)

    def halves(d):
        hi = d.astype(jnp.bfloat16)
        return hi, (d - hi.astype(jnp.float32)).astype(jnp.bfloat16)

    def split(i):
        load(i).wait()
        d = dbuf[pl.ds(i * DCH, DCH), :]
        hi, lo = halves(d)
        ds[pl.ds(i * DCH, DCH), 0:K] = hi
        ds[pl.ds(i * DCH, DCH), K:2 * K] = lo
        p = d[:, 0:W] * d[:, 0:W]
        for c in range(1, K // W):
            q = d[:, c * W:(c + 1) * W]
            p = p + q * q
        for c in range(DCH // W):
            row = jnp.sum(p[c * W:(c + 1) * W].T, axis=0, keepdims=True)
            sq[i * (DCH // W) + c:i * (DCH // W) + c + 1, :] = row

    sent, due = [], {}

    def go(make, *key):
        copy = make(*key)
        copy.start()
        sent.append(copy)
        due[(make,) + key] = copy

    def got(make, *key):
        due.pop((make,) + key).wait_recv()

    def near_start(g):
        if g in Y_FIRST:
            for j in range(3):
                got(row_send, g, j)
        for i in range(4):
            go(near_send, g, i)

    def on_start(g):
        for i in range(4):
            got(near_send, g, i)
        for i in range(3):
            go(on_send, g, i)

    def on_wait(g):
        for i in range(3):
            got(on_send, g, i)

    def rows_start(g):
        for j in range(3):
            go(row_send, g, j)

    def columns_start(g):
        on_wait(g)
        for way in (PLUS, MINUS):
            go(column_send, g, way)

    def halves_start(g):
        for way in (PLUS, MINUS):
            got(column_send, g, way)
            go(half_send, g, way)

    def halves_wait(g):
        for way in (PLUS, MINUS):
            got(half_send, g, way)

    def panel_part(u, a):
        hi, lo = halves(jnp.concatenate([land[u, a, k] for k in range(NY)], axis=0))
        for off in (0, K):
            rows = pl.ds(pl.multiple_of(off + a * (NY * SHARD), 16), NY * SHARD)
            rhs[u, rows, 0:W] = hi
            rhs[u, rows, W:2 * W] = lo

    def panel(u):
        for a in range(NZ):
            panel_part(u, a)

    def dot(left, u):
        full = jnp.dot(left, rhs[u], preferred_element_type=jnp.float32)
        return full[:, 0:W] + full[:, W:2 * W]

    def product(u, r, n):
        return dot(ds[pl.ds(r, n), :], u)

    barrier = pltpu.get_barrier_semaphore()
    peers = [at_z(d) for d in ZS] + [at_y(d) for d in YS] + [at_x(d) for d in XS] + [{"tgt": 1 - core}]
    for peer in peers:
        pl.semaphore_signal(barrier, inc=1, device_id=peer, device_id_type=MESH)
    for u in OWN:
        own_piece(u).start()
    pl.semaphore_wait(barrier, len(peers))

    for i in range(NZ - 1):
        go(z_send, i)
    for i in range(len(PIECES)):
        go(piece_send, i)
    for way in (PLUS, MINUS):
        go(pair_send, way)
    for u in OWN:
        own_piece(u).wait()
    rows_start(2)
    for j in range(3):
        go(first_send, NZ - 1, j)
    near_start(1)
    for i in range(ROWS // DCH):
        load(i).start()
    for i in range(0, 4):
        split(i)
    for i in range(NZ - 1):
        got(z_send, i)
        for j in range(3):
            go(first_send, i, j)
        if i == 3:
            near_start(2)
        if i == 5:
            on_start(1)
    for i in range(len(PIECES)):
        got(piece_send, i)
    near_start(3)
    near_start(4)
    rows_start(5)
    for i in range(4, 8):
        split(i)
    for i in range(3):
        go(sq_send, i)
    columns_start(1)
    for i in (NZ - 1,) + tuple(range(NZ - 1)):
        for j in range(3):
            got(first_send, i, j)
        panel_part(0, z if i == NZ - 1 else lax.rem(z + NZ - ZS[i], NZ))

    for b, (r, n) in enumerate(BLOCKS):
        for way, base in ((PLUS, HALF), (MINUS, 0)):
            out_x[FAR, way, pl.ds(r, n), :] = product(0, base + r, n)
            go(x_send, FAR, way, b)
        if b == 0:
            on_start(2)
    on_start(3)
    on_start(4)
    halves_start(1)
    halves_wait(1)
    panel(1)
    on_wait(2)
    panel(2)
    for b, (r, n) in enumerate(BLOCKS):
        for way, base, u in ((PLUS, 0, 1), (MINUS, HALF, 2)):
            out_x[NEAR, way, pl.ds(r, n), :] = product(u, base + r, n)
            go(x_send, NEAR, way, b)
        if b == 1:
            columns_start(3)
            near_start(5)
            columns_start(4)
    for way in (PLUS, MINUS):
        got(pair_send, way)
    go(pair_share)
    halves_start(3)
    on_start(5)
    for b, (r, n) in enumerate(BLOCKS):
        for way, base, u in ((PLUS, HALF, 1), (MINUS, 0, 2)):
            mine = product(u, base + r, n)
            got(x_send, FAR, way, b)
            out_x[SUM, way, pl.ds(r, n), :] = mine + in_x[FAR, way, pl.ds(r, n), :]
            go(x_send, SUM, way, b)

    got(pair_share)
    for which in range(2):
        for c in range(2):
            hi, lo = halves(car[c, which])
            cds[which, c * PART:(c + 1) * PART, 0:K] = hi
            cds[which, c * PART:(c + 1) * PART, K:2 * K] = lo
    halves_start(4)
    halves_wait(3)
    panel(3)
    panel(4)
    for way, which, mine, theirs in ((PLUS, 1, 1, 4), (MINUS, 0, 2, 3)):
        out_p[way] = dot(ds[pair_rows(which), :], mine) + dot(cds[which], theirs)
        go(pair_sum_send, way)
    for i in range(3):
        got(sq_send, i)
    inverse = lax.rsqrt(sq[...] + sqin[0] + sqin[1] + sqin[2] + EPS)
    for i in range(ROWS // W):
        scale[i * W:(i + 1) * W, :] = jnp.broadcast_to(inverse[i:i + 1, :], (W, W)).T
    halves_wait(4)
    on_wait(5)
    for u in (5, 6, 7):
        panel(u)
    for r in range(0, KEPT, 256):
        n = min(256, KEPT - r)
        o_ref[pl.ds(r, n), :] = product(5, r, n)
    for which in range(2):
        o_ref[pair_rows(which), :] = dot(ds[pair_rows(which), :], 5) + dot(cds[which], 6 + which)

    for b, (r, n) in enumerate(BLOCKS):
        got(x_send, NEAR, PLUS, b)
        got(x_send, NEAR, MINUS, b)
        for way, base, near in ((PLUS, HALF, MINUS), (MINUS, 0, PLUS)):
            got(x_send, SUM, way, b)
            rows = pl.ds(base + r, n)
            o_ref[rows, :] = (o_ref[rows, :] + in_x[NEAR, near, pl.ds(r, n), :]
                              + in_x[SUM, way, pl.ds(r, n), :]) * scale[rows, :]
    for way, which in ((PLUS, 0), (MINUS, 1)):
        got(pair_sum_send, way)
        rows = pair_rows(which)
        o_ref[rows, :] = (o_ref[rows, :] + in_p[way]) * scale[rows, :]

    for copy in due.values():
        copy.wait_recv()
    for copy in sent:
        copy.wait_send()


def shards(decoder_slab, encoder_panel):
    f32, bf16 = jnp.float32, jnp.bfloat16
    dma = pltpu.SemaphoreType.DMA
    ng = len(GROUPS)
    out = pl.pallas_call(
        kernel,
        out_shape=pltpu.VMEM((ROWS, W), f32),
        in_specs=[pl.BlockSpec(memory_space=pl.ANY)] * 2,
        out_specs=pl.BlockSpec(memory_space=pltpu.VMEM),
        scratch_shapes=[
            pltpu.VMEM((ROWS, K), f32),
            pltpu.VMEM((ROWS, 2 * K), bf16),
            pltpu.VMEM((8, NZ, NY, SHARD, W), f32),
            pltpu.VMEM((8, 2 * K, 2 * W), bf16),
            pltpu.VMEM((ROWS // W, W), f32),
            pltpu.VMEM((3, ROWS // W, W), f32),
            pltpu.VMEM((ROWS, W), f32),
            pltpu.VMEM((3, 2, HALF, W), f32),
            pltpu.VMEM((3, 2, HALF, W), f32),
            pltpu.VMEM((2, PAIR, W), f32),
            pltpu.VMEM((2, PAIR, W), f32),
            pltpu.VMEM((2, 2, PART, K), f32),
            pltpu.VMEM((2, PAIR, 2 * K), bf16),
            dma((ROWS // DCH,)), dma((8,)),
            dma((len(PIECES),)), dma((len(PIECES),)),
            dma((NZ - 1,)), dma((NZ - 1,)),
            dma((NZ, 3)), dma((NZ, 3)),
            dma((ng, 4)), dma((ng, 4)),
            dma((ng, 3)), dma((ng, 3)),
            dma((ng, 3)), dma((ng, 3)),
            dma((ng, 2)), dma((ng, 2)),
            dma((3, 2, NB)), dma((3, 2, NB)),
            dma((3,)), dma((3,)),
            dma((3,)), dma((3,)),
            dma((2,)), dma((2,)),
        ],
        compiler_params=pltpu.CompilerParams(
            collective_id=0, has_side_effects=True, vmem_limit_bytes=56 * 1024 * 1024),
    )(decoder_slab, encoder_panel)
    return out.reshape(ROWS, 1, W)


def solution(mesh):
    placed = (P("src", "hid"), P(("hid", "src"), "tgt"))
    return jax.shard_map(
        shards, mesh=mesh, in_specs=placed, out_specs=P("src", "tgt", "hid"), check_vma=False
    )
```

```python
import jax
import jax.numpy as jnp
from jax import lax
from jax.experimental import pallas as pl
from jax.experimental.pallas import tpu as pltpu
from jax.sharding import PartitionSpec as P

EPS = 1e-06
MESH = pl.DeviceIdType.MESH
NX, NY, NZ = 4, 4, 8
ROWS, K, W = 2048, 896, 128
SHARD = K // (NY * NZ)
PAIR = 224
PART = PAIR // 2
KEPT = ROWS - 2 * PAIR
HALF = KEPT // 2
BLOCKS = ((0, 128), (128, 272), (400, 272), (672, 128))
NB = len(BLOCKS)
DCH = 256
ZS = (1, 7, 2, 6, 3, 5, 4)
YS = (2, 1, 3)
XS = (2, 1, 3)
OWN = {0: 2, 1: 1, 2: 3, 5: 0}
PIECES = ((4, 2, 1), (3, 2, 3), (7, 1, 1), (6, 3, 3))
GROUPS = ((0, 1), (1, 1), (2, 1), (3, 2), (5, 2), (7, 1))
Y_FIRST = (2, 5)
FAR, NEAR, SUM = 0, 1, 2
PLUS, MINUS = 0, 1


def kernel(d_ref, e_ref, o_ref, dbuf, ds, land, rhs, sq, sqin, scale, out_x, in_x, out_p, in_p, car, cds,
           dsem, esem, pss, prs, zss, zrs, yss, yrs, uss, urs, vss, vrs, wss, wrs, fss, frs, xss, xrs, qss, qrs, css, crs, ass, ars):
    h = lax.axis_index("hid")
    s = lax.axis_index("src")
    core = lax.axis_index("tgt")
    z, y = s // NY, lax.rem(s, NY)
    odd = lax.rem(h, 2)
    pairs = (KEPT + odd * PAIR, KEPT + (1 - odd) * PAIR)

    def at_x(d):
        return {"hid": lax.rem(h + d, NX)}

    def at_z(d):
        return {"src": lax.rem(z + d, NZ) * NY + y}

    def at_y(d):
        return {"src": z * NY + lax.rem(y + d, NY)}

    def remote(src, dst, send, recv, peer):
        return pltpu.make_async_remote_copy(
            src_ref=src, dst_ref=dst, send_sem=send, recv_sem=recv, device_id=peer, device_id_type=MESH)

    def load(i):
        return pltpu.make_async_copy(
            d_ref.at[pl.ds(i * DCH, DCH)], dbuf.at[pl.ds(i * DCH, DCH)], dsem.at[i])

    def columns(d):
        t = lax.rem(h + d, NX)
        return e_ref.at[:, pl.ds(pl.multiple_of(t * W, W), W)]

    def own_piece(u):
        return pltpu.make_async_copy(columns(OWN[u]), land.at[u, z, y], esem.at[u])

    def piece_send(i):
        unit, d, peer = PIECES[i]
        return remote(columns(d), land.at[unit, z, y], pss.at[i], prs.at[i], at_x(peer))

    def z_send(i):
        return remote(columns(OWN[0]), land.at[0, z, y], zss.at[i], zrs.at[i], at_z(ZS[i]))

    def bundle(g, zz):
        return land.at[pl.ds(*GROUPS[g]), zz] if g in Y_FIRST else land.at[pl.ds(*GROUPS[g]), zz, y]

    def near_send(g, i):
        part = bundle(g, z)
        return remote(part, part, uss.at[g, i], urs.at[g, i], at_z((2, 6, 1, 7)[i]))

    def on_send(g, i):
        came, to = ((6, 1), (2, 7), (6 + 4 * core, 2 + 4 * core))[i]
        part = bundle(g, lax.rem(z + came, NZ))
        return remote(part, part, vss.at[g, i], vrs.at[g, i], at_z(to))

    def row_send(g, j):
        part = land.at[pl.ds(*GROUPS[g]), z, y]
        return remote(part, part, wss.at[g, j], wrs.at[g, j], at_y(YS[j]))

    def first_send(i, j):
        zz = z if i == NZ - 1 else lax.rem(z + NZ - ZS[i], NZ)
        return remote(land.at[0, zz, y], land.at[0, zz, y], yss.at[i, j], yrs.at[i, j], at_y(YS[j]))

    def column_send(g, way):
        part = land.at[pl.ds(*GROUPS[g]), :, y]
        return remote(part, part, wss.at[g, way], wrs.at[g, way], at_y(1 if way == PLUS else 3))

    def half_send(g, way):
        yy = lax.rem(y + (3 if way == PLUS else 1), NY)
        part = land.at[pl.ds(*GROUPS[g]), pl.ds(0 if way == PLUS else NZ // 2, NZ // 2), yy]
        return remote(part, part, fss.at[g, way], frs.at[g, way], at_y(1 if way == PLUS else 3))

    def sq_send(i):
        return remote(sq, sqin.at[i], qss.at[i], qrs.at[i], at_x(XS[i]))

    def x_send(part, way, b):
        rows = pl.ds(*BLOCKS[b])
        return remote(out_x.at[part, way, rows], in_x.at[part, way, rows], xss.at[part, way, b],
                      xrs.at[part, way, b], at_x(1 if way == PLUS else 3))

    def pair_send(way):
        r = pl.multiple_of(pairs[way] + core * PART, 16)
        return remote(d_ref.at[pl.ds(r, PART)], car.at[core, 1 - way], css.at[way], crs.at[way],
                      at_x(1 if way == PLUS else 3))

    def pair_share():
        return remote(car.at[core], car.at[core], css.at[2], crs.at[2], {"tgt": 1 - core})

    def pair_sum_send(way):
        return remote(out_p.at[way], in_p.at[way], ass.at[way], ars.at[way], at_x(1 if way == PLUS else 3))

    def pair_rows(which):
        return pl.ds(pl.multiple_of(pairs[which], 16), PAIR)

    def halves(d):
        hi = d.astype(jnp.bfloat16)
        return hi, (d - hi.astype(jnp.float32)).astype(jnp.bfloat16)

    def split(i):
        load(i).wait()
        d = dbuf[pl.ds(i * DCH, DCH), :]
        hi, lo = halves(d)
        ds[pl.ds(i * DCH, DCH), 0:K] = hi
        ds[pl.ds(i * DCH, DCH), K:2 * K] = lo
        p = d[:, 0:W] * d[:, 0:W]
        for c in range(1, K // W):
            q = d[:, c * W:(c + 1) * W]
            p = p + q * q
        for c in range(DCH // W):
            row = jnp.sum(p[c * W:(c + 1) * W].T, axis=0, keepdims=True)
            sq[i * (DCH // W) + c:i * (DCH // W) + c + 1, :] = row

    sent, due = [], {}

    def go(make, *key):
        copy = make(*key)
        copy.start()
        sent.append(copy)
        due[(make,) + key] = copy

    def got(make, *key):
        due.pop((make,) + key).wait_recv()

    def near_start(g):
        if g in Y_FIRST:
            for j in range(3):
                got(row_send, g, j)
        for i in range(4):
            go(near_send, g, i)

    def on_start(g):
        for i in range(4):
            got(near_send, g, i)
        for i in range(3):
            go(on_send, g, i)

    def on_wait(g):
        for i in range(3):
            got(on_send, g, i)

    def rows_start(g):
        for j in range(3):
            go(row_send, g, j)

    def columns_start(g):
        on_wait(g)
        for way in (PLUS, MINUS):
            go(column_send, g, way)

    def halves_start(g):
        for way in (PLUS, MINUS):
            got(column_send, g, way)
            go(half_send, g, way)

    def halves_wait(g):
        for way in (PLUS, MINUS):
            got(half_send, g, way)

    def panel_part(u, a):
        hi, lo = halves(jnp.concatenate([land[u, a, k] for k in range(NY)], axis=0))
        for off in (0, K):
            rows = pl.ds(pl.multiple_of(off + a * (NY * SHARD), 16), NY * SHARD)
            rhs[u, rows, 0:W] = hi
            rhs[u, rows, W:2 * W] = lo

    def panel(u):
        for a in range(NZ):
            panel_part(u, a)

    def dot(left, u):
        full = jnp.dot(left, rhs[u], preferred_element_type=jnp.float32)
        return full[:, 0:W] + full[:, W:2 * W]

    def product(u, r, n):
        return dot(ds[pl.ds(r, n), :], u)

    barrier = pltpu.get_barrier_semaphore()
    peers = [at_z(d) for d in ZS] + [at_y(d) for d in YS] + [at_x(d) for d in XS] + [{"tgt": 1 - core}]
    for peer in peers:
        pl.semaphore_signal(barrier, inc=1, device_id=peer, device_id_type=MESH)
    for u in OWN:
        own_piece(u).start()
    pl.semaphore_wait(barrier, len(peers))

    for i in range(NZ - 1):
        go(z_send, i)
    for i in range(len(PIECES)):
        go(piece_send, i)
    for way in (PLUS, MINUS):
        go(pair_send, way)
    for u in OWN:
        own_piece(u).wait()
    rows_start(2)
    for j in range(3):
        go(first_send, NZ - 1, j)
    near_start(1)
    for i in range(ROWS // DCH):
        load(i).start()
    for i in range(0, 4):
        split(i)
    for i in range(NZ - 1):
        got(z_send, i)
        for j in range(3):
            go(first_send, i, j)
        if i == 3:
            near_start(2)
        if i == 5:
            on_start(1)
    for i in range(len(PIECES)):
        got(piece_send, i)
    near_start(3)
    near_start(4)
    rows_start(5)
    for i in range(4, 8):
        split(i)
    for i in range(3):
        go(sq_send, i)
    for i in (NZ - 1,) + tuple(range(NZ - 1)):
        for j in range(3):
            got(first_send, i, j)
        panel_part(0, z if i == NZ - 1 else lax.rem(z + NZ - ZS[i], NZ))

    for b, (r, n) in enumerate(BLOCKS):
        for way, base in ((PLUS, HALF), (MINUS, 0)):
            out_x[FAR, way, pl.ds(r, n), :] = product(0, base + r, n)
            go(x_send, FAR, way, b)
        if b == 0:
            columns_start(1)
            on_start(2)
    on_start(3)
    on_start(4)
    halves_start(1)
    halves_wait(1)
    panel(1)
    on_wait(2)
    panel(2)
    for b, (r, n) in enumerate(BLOCKS):
        for way, base, u in ((PLUS, 0, 1), (MINUS, HALF, 2)):
            out_x[NEAR, way, pl.ds(r, n), :] = product(u, base + r, n)
            go(x_send, NEAR, way, b)
        if b == 1:
            columns_start(3)
            near_start(5)
            columns_start(4)
    for way in (PLUS, MINUS):
        got(pair_send, way)
    go(pair_share)
    halves_start(3)
    on_start(5)
    for b, (r, n) in enumerate(BLOCKS):
        for way, base, u in ((PLUS, HALF, 1), (MINUS, 0, 2)):
            mine = product(u, base + r, n)
            got(x_send, FAR, way, b)
            out_x[SUM, way, pl.ds(r, n), :] = mine + in_x[FAR, way, pl.ds(r, n), :]
            go(x_send, SUM, way, b)

    got(pair_share)
    for which in range(2):
        for c in range(2):
            hi, lo = halves(car[c, which])
            cds[which, c * PART:(c + 1) * PART, 0:K] = hi
            cds[which, c * PART:(c + 1) * PART, K:2 * K] = lo
    halves_start(4)
    halves_wait(3)
    panel(3)
    panel(4)
    for way, which, mine, theirs in ((PLUS, 1, 1, 4), (MINUS, 0, 2, 3)):
        out_p[way] = dot(ds[pair_rows(which), :], mine) + dot(cds[which], theirs)
        go(pair_sum_send, way)
    for i in range(3):
        got(sq_send, i)
    inverse = lax.rsqrt(sq[...] + sqin[0] + sqin[1] + sqin[2] + EPS)
    for i in range(ROWS // W):
        scale[i * W:(i + 1) * W, :] = jnp.broadcast_to(inverse[i:i + 1, :], (W, W)).T
    halves_wait(4)
    on_wait(5)
    for u in (5, 6, 7):
        panel(u)
    for r in range(0, KEPT, 256):
        n = min(256, KEPT - r)
        o_ref[pl.ds(r, n), :] = product(5, r, n)
    for which in range(2):
        o_ref[pair_rows(which), :] = dot(ds[pair_rows(which), :], 5) + dot(cds[which], 6 + which)

    for b, (r, n) in enumerate(BLOCKS):
        got(x_send, NEAR, PLUS, b)
        got(x_send, NEAR, MINUS, b)
        for way, base, near in ((PLUS, HALF, MINUS), (MINUS, 0, PLUS)):
            got(x_send, SUM, way, b)
            rows = pl.ds(base + r, n)
            o_ref[rows, :] = (o_ref[rows, :] + in_x[NEAR, near, pl.ds(r, n), :]
                              + in_x[SUM, way, pl.ds(r, n), :]) * scale[rows, :]
    for way, which in ((PLUS, 0), (MINUS, 1)):
        got(pair_sum_send, way)
        rows = pair_rows(which)
        o_ref[rows, :] = (o_ref[rows, :] + in_p[way]) * scale[rows, :]

    for copy in due.values():
        copy.wait_recv()
    for copy in sent:
        copy.wait_send()


def shards(decoder_slab, encoder_panel):
    f32, bf16 = jnp.float32, jnp.bfloat16
    dma = pltpu.SemaphoreType.DMA
    ng = len(GROUPS)
    out = pl.pallas_call(
        kernel,
        out_shape=pltpu.VMEM((ROWS, W), f32),
        in_specs=[pl.BlockSpec(memory_space=pl.ANY)] * 2,
        out_specs=pl.BlockSpec(memory_space=pltpu.VMEM),
        scratch_shapes=[
            pltpu.VMEM((ROWS, K), f32),
            pltpu.VMEM((ROWS, 2 * K), bf16),
            pltpu.VMEM((8, NZ, NY, SHARD, W), f32),
            pltpu.VMEM((8, 2 * K, 2 * W), bf16),
            pltpu.VMEM((ROWS // W, W), f32),
            pltpu.VMEM((3, ROWS // W, W), f32),
            pltpu.VMEM((ROWS, W), f32),
            pltpu.VMEM((3, 2, HALF, W), f32),
            pltpu.VMEM((3, 2, HALF, W), f32),
            pltpu.VMEM((2, PAIR, W), f32),
            pltpu.VMEM((2, PAIR, W), f32),
            pltpu.VMEM((2, 2, PART, K), f32),
            pltpu.VMEM((2, PAIR, 2 * K), bf16),
            dma((ROWS // DCH,)), dma((8,)),
            dma((len(PIECES),)), dma((len(PIECES),)),
            dma((NZ - 1,)), dma((NZ - 1,)),
            dma((NZ, 3)), dma((NZ, 3)),
            dma((ng, 4)), dma((ng, 4)),
            dma((ng, 3)), dma((ng, 3)),
            dma((ng, 3)), dma((ng, 3)),
            dma((ng, 2)), dma((ng, 2)),
            dma((3, 2, NB)), dma((3, 2, NB)),
            dma((3,)), dma((3,)),
            dma((3,)), dma((3,)),
            dma((2,)), dma((2,)),
        ],
        compiler_params=pltpu.CompilerParams(
            collective_id=0, has_side_effects=True, vmem_limit_bytes=56 * 1024 * 1024),
    )(decoder_slab, encoder_panel)
    return out.reshape(ROWS, 1, W)


def solution(mesh):
    placed = (P("src", "hid"), P(("hid", "src"), "tgt"))
    return jax.shard_map(
        shards, mesh=mesh, in_specs=placed, out_specs=P("src", "tgt", "hid"), check_vma=False
    )
```

```python
import jax
import jax.numpy as jnp
from jax import lax
from jax.experimental import pallas as pl
from jax.experimental.pallas import tpu as pltpu
from jax.sharding import PartitionSpec as P

EPS = 1e-06
MESH = pl.DeviceIdType.MESH
NX, NY, NZ = 4, 4, 8
ROWS, K, W = 2048, 896, 128
SHARD = K // (NY * NZ)
PAIR = 224
PART = PAIR // 2
KEPT = ROWS - 2 * PAIR
HALF = KEPT // 2
BLOCKS = ((0, 128), (128, 272), (400, 272), (672, 128))
NB = len(BLOCKS)
DCH = 256
ZS = (1, 7, 2, 6, 3, 5, 4)
YS = (2, 1, 3)
XS = (2, 1, 3)
OWN = {0: 2, 1: 1, 2: 3, 5: 0}
PIECES = ((4, 2, 1), (3, 2, 3), (7, 1, 1), (6, 3, 3))
GROUPS = ((0, 1), (1, 1), (2, 1), (3, 2), (5, 2), (7, 1))
Y_FIRST = (2, 5)
FAR, NEAR, SUM = 0, 1, 2
PLUS, MINUS = 0, 1


def kernel(d_ref, e_ref, o_ref, dbuf, ds, land, rhs, sq, sqin, scale, out_x, in_x, out_p, in_p, car, cds,
           dsem, esem, pss, prs, zss, zrs, yss, yrs, uss, urs, vss, vrs, wss, wrs, fss, frs, xss, xrs, qss, qrs, css, crs, ass, ars):
    h = lax.axis_index("hid")
    s = lax.axis_index("src")
    core = lax.axis_index("tgt")
    z, y = s // NY, lax.rem(s, NY)
    odd = lax.rem(h, 2)
    pairs = (KEPT + odd * PAIR, KEPT + (1 - odd) * PAIR)

    def at_x(d):
        return {"hid": lax.rem(h + d, NX)}

    def at_z(d):
        return {"src": lax.rem(z + d, NZ) * NY + y}

    def at_y(d):
        return {"src": z * NY + lax.rem(y + d, NY)}

    def remote(src, dst, send, recv, peer):
        return pltpu.make_async_remote_copy(
            src_ref=src, dst_ref=dst, send_sem=send, recv_sem=recv, device_id=peer, device_id_type=MESH)

    def load(i):
        return pltpu.make_async_copy(
            d_ref.at[pl.ds(i * DCH, DCH)], dbuf.at[pl.ds(i * DCH, DCH)], dsem.at[i])

    def columns(d):
        t = lax.rem(h + d, NX)
        return e_ref.at[:, pl.ds(pl.multiple_of(t * W, W), W)]

    def own_piece(u):
        return pltpu.make_async_copy(columns(OWN[u]), land.at[u, z, y], esem.at[u])

    def piece_send(i):
        unit, d, peer = PIECES[i]
        return remote(columns(d), land.at[unit, z, y], pss.at[i], prs.at[i], at_x(peer))

    def z_send(i):
        return remote(columns(OWN[0]), land.at[0, z, y], zss.at[i], zrs.at[i], at_z(ZS[i]))

    def bundle(g, zz):
        return land.at[pl.ds(*GROUPS[g]), zz] if g in Y_FIRST else land.at[pl.ds(*GROUPS[g]), zz, y]

    def near_send(g, i):
        part = bundle(g, z)
        return remote(part, part, uss.at[g, i], urs.at[g, i], at_z((2, 6, 1, 7)[i]))

    def on_send(g, i):
        came, to = ((6, 1), (2, 7), (6 + 4 * core, 2 + 4 * core))[i]
        part = bundle(g, lax.rem(z + came, NZ))
        return remote(part, part, vss.at[g, i], vrs.at[g, i], at_z(to))

    def row_send(g, j):
        part = land.at[pl.ds(*GROUPS[g]), z, y]
        return remote(part, part, wss.at[g, j], wrs.at[g, j], at_y(YS[j]))

    def first_send(i, j):
        zz = z if i == NZ - 1 else lax.rem(z + NZ - ZS[i], NZ)
        return remote(land.at[0, zz, y], land.at[0, zz, y], yss.at[i, j], yrs.at[i, j], at_y(YS[j]))

    def column_send(g, way):
        part = land.at[pl.ds(*GROUPS[g]), :, y]
        return remote(part, part, wss.at[g, way], wrs.at[g, way], at_y(1 if way == PLUS else 3))

    def half_send(g, way):
        yy = lax.rem(y + (3 if way == PLUS else 1), NY)
        part = land.at[pl.ds(*GROUPS[g]), pl.ds(0 if way == PLUS else NZ // 2, NZ // 2), yy]
        return remote(part, part, fss.at[g, way], frs.at[g, way], at_y(1 if way == PLUS else 3))

    def sq_send(i):
        return remote(sq, sqin.at[i], qss.at[i], qrs.at[i], at_x(XS[i]))

    def x_send(part, way, b):
        rows = pl.ds(*BLOCKS[b])
        return remote(out_x.at[part, way, rows], in_x.at[part, way, rows], xss.at[part, way, b],
                      xrs.at[part, way, b], at_x(1 if way == PLUS else 3))

    def pair_send(way):
        r = pl.multiple_of(pairs[way] + core * PART, 16)
        return remote(d_ref.at[pl.ds(r, PART)], car.at[core, 1 - way], css.at[way], crs.at[way],
                      at_x(1 if way == PLUS else 3))

    def pair_share():
        return remote(car.at[core], car.at[core], css.at[2], crs.at[2], {"tgt": 1 - core})

    def pair_sum_send(way):
        return remote(out_p.at[way], in_p.at[way], ass.at[way], ars.at[way], at_x(1 if way == PLUS else 3))

    def pair_rows(which):
        return pl.ds(pl.multiple_of(pairs[which], 16), PAIR)

    def halves(d):
        hi = d.astype(jnp.bfloat16)
        return hi, (d - hi.astype(jnp.float32)).astype(jnp.bfloat16)

    def split(i):
        load(i).wait()
        d = dbuf[pl.ds(i * DCH, DCH), :]
        hi, lo = halves(d)
        ds[pl.ds(i * DCH, DCH), 0:K] = hi
        ds[pl.ds(i * DCH, DCH), K:2 * K] = lo
        p = d[:, 0:W] * d[:, 0:W]
        for c in range(1, K // W):
            q = d[:, c * W:(c + 1) * W]
            p = p + q * q
        for c in range(DCH // W):
            row = jnp.sum(p[c * W:(c + 1) * W].T, axis=0, keepdims=True)
            sq[i * (DCH // W) + c:i * (DCH // W) + c + 1, :] = row

    sent, due = [], {}

    def go(make, *key):
        copy = make(*key)
        copy.start()
        sent.append(copy)
        due[(make,) + key] = copy

    def got(make, *key):
        due.pop((make,) + key).wait_recv()

    def near_start(g):
        if g in Y_FIRST:
            for j in range(3):
                got(row_send, g, j)
        for i in range(4):
            go(near_send, g, i)

    def on_start(g):
        for i in range(4):
            got(near_send, g, i)
        for i in range(3):
            go(on_send, g, i)

    def on_wait(g):
        for i in range(3):
            got(on_send, g, i)

    def rows_start(g):
        for j in range(3):
            go(row_send, g, j)

    def columns_start(g):
        on_wait(g)
        for way in (PLUS, MINUS):
            go(column_send, g, way)

    def halves_start(g):
        for way in (PLUS, MINUS):
            got(column_send, g, way)
            go(half_send, g, way)

    def halves_wait(g):
        for way in (PLUS, MINUS):
            got(half_send, g, way)

    def panel_part(u, a):
        hi, lo = halves(jnp.concatenate([land[u, a, k] for k in range(NY)], axis=0))
        for off in (0, K):
            rows = pl.ds(pl.multiple_of(off + a * (NY * SHARD), 16), NY * SHARD)
            rhs[u, rows, 0:W] = hi
            rhs[u, rows, W:2 * W] = lo

    def panel(u):
        for a in range(NZ):
            panel_part(u, a)

    def dot(left, u):
        full = jnp.dot(left, rhs[u], preferred_element_type=jnp.float32)
        return full[:, 0:W] + full[:, W:2 * W]

    def product(u, r, n):
        return dot(ds[pl.ds(r, n), :], u)

    barrier = pltpu.get_barrier_semaphore()
    peers = [at_z(d) for d in ZS] + [at_y(d) for d in YS] + [at_x(d) for d in XS] + [{"tgt": 1 - core}]
    for peer in peers:
        pl.semaphore_signal(barrier, inc=1, device_id=peer, device_id_type=MESH)
    for u in OWN:
        own_piece(u).start()
    pl.semaphore_wait(barrier, len(peers))

    for i in range(NZ - 1):
        go(z_send, i)
    for i in range(len(PIECES)):
        go(piece_send, i)
    for way in (PLUS, MINUS):
        go(pair_send, way)
    for u in OWN:
        own_piece(u).wait()
    rows_start(2)
    for j in range(3):
        go(first_send, NZ - 1, j)
    near_start(1)
    for i in range(ROWS // DCH):
        load(i).start()
    for i in range(0, 4):
        split(i)
    for i in range(NZ - 1):
        got(z_send, i)
        for j in range(3):
            go(first_send, i, j)
        if i == 3:
            near_start(2)
        if i == 5:
            on_start(1)
    for i in range(len(PIECES)):
        got(piece_send, i)
    near_start(3)
    near_start(4)
    rows_start(5)
    for i in range(4, 8):
        split(i)
    for i in range(3):
        go(sq_send, i)
    for i in (NZ - 1,) + tuple(range(NZ - 1)):
        for j in range(3):
            got(first_send, i, j)
        panel_part(0, z if i == NZ - 1 else lax.rem(z + NZ - ZS[i], NZ))

    for b, (r, n) in enumerate(BLOCKS):
        for way, base in ((PLUS, HALF), (MINUS, 0)):
            out_x[FAR, way, pl.ds(r, n), :] = product(0, base + r, n)
            go(x_send, FAR, way, b)
        if b == 0:
            columns_start(1)
            on_start(2)
    on_start(3)
    on_start(4)
    halves_start(1)
    halves_wait(1)
    panel(1)
    on_wait(2)
    panel(2)
    for b, (r, n) in enumerate(BLOCKS):
        for way, base, u in ((PLUS, 0, 1), (MINUS, HALF, 2)):
            out_x[NEAR, way, pl.ds(r, n), :] = product(u, base + r, n)
            go(x_send, NEAR, way, b)
        if b == 1:
            columns_start(3)
            near_start(5)
            columns_start(4)
    for way in (PLUS, MINUS):
        got(pair_send, way)
    go(pair_share)
    halves_start(3)
    on_start(5)
    for b, (r, n) in enumerate(BLOCKS):
        for way, base, u in ((PLUS, HALF, 1), (MINUS, 0, 2)):
            mine = product(u, base + r, n)
            got(x_send, FAR, way, b)
            out_x[SUM, way, pl.ds(r, n), :] = mine + in_x[FAR, way, pl.ds(r, n), :]
            go(x_send, SUM, way, b)

    got(pair_share)
    for which in range(2):
        for c in range(2):
            hi, lo = halves(car[c, which])
            cds[which, c * PART:(c + 1) * PART, 0:K] = hi
            cds[which, c * PART:(c + 1) * PART, K:2 * K] = lo
    halves_start(4)
    halves_wait(3)
    panel(3)
    panel(4)
    for way, which, mine, theirs in ((PLUS, 1, 1, 4), (MINUS, 0, 2, 3)):
        out_p[way] = dot(ds[pair_rows(which), :], mine) + dot(cds[which], theirs)
        go(pair_sum_send, way)
    for i in range(3):
        got(sq_send, i)
    inverse = lax.rsqrt(sq[...] + sqin[0] + sqin[1] + sqin[2] + EPS)
    for i in range(ROWS // W):
        scale[i * W:(i + 1) * W, :] = jnp.broadcast_to(inverse[i:i + 1, :], (W, W)).T
    halves_wait(4)
    panel(5)
    for r in range(0, KEPT, 256):
        n = min(256, KEPT - r)
        o_ref[pl.ds(r, n), :] = product(5, r, n)
    on_wait(5)
    for which in range(2):
        panel(6 + which)
        o_ref[pair_rows(which), :] = dot(ds[pair_rows(which), :], 5) + dot(cds[which], 6 + which)

    for b, (r, n) in enumerate(BLOCKS):
        got(x_send, NEAR, PLUS, b)
        got(x_send, NEAR, MINUS, b)
        for way, base, near in ((PLUS, HALF, MINUS), (MINUS, 0, PLUS)):
            got(x_send, SUM, way, b)
            rows = pl.ds(base + r, n)
            o_ref[rows, :] = (o_ref[rows, :] + in_x[NEAR, near, pl.ds(r, n), :]
                              + in_x[SUM, way, pl.ds(r, n), :]) * scale[rows, :]
    for way, which in ((PLUS, 0), (MINUS, 1)):
        got(pair_sum_send, way)
        rows = pair_rows(which)
        o_ref[rows, :] = (o_ref[rows, :] + in_p[way]) * scale[rows, :]

    for copy in due.values():
        copy.wait_recv()
    for copy in sent:
        copy.wait_send()


def shards(decoder_slab, encoder_panel):
    f32, bf16 = jnp.float32, jnp.bfloat16
    dma = pltpu.SemaphoreType.DMA
    ng = len(GROUPS)
    out = pl.pallas_call(
        kernel,
        out_shape=pltpu.VMEM((ROWS, W), f32),
        in_specs=[pl.BlockSpec(memory_space=pl.ANY)] * 2,
        out_specs=pl.BlockSpec(memory_space=pltpu.VMEM),
        scratch_shapes=[
            pltpu.VMEM((ROWS, K), f32),
            pltpu.VMEM((ROWS, 2 * K), bf16),
            pltpu.VMEM((8, NZ, NY, SHARD, W), f32),
            pltpu.VMEM((8, 2 * K, 2 * W), bf16),
            pltpu.VMEM((ROWS // W, W), f32),
            pltpu.VMEM((3, ROWS // W, W), f32),
            pltpu.VMEM((ROWS, W), f32),
            pltpu.VMEM((3, 2, HALF, W), f32),
            pltpu.VMEM((3, 2, HALF, W), f32),
            pltpu.VMEM((2, PAIR, W), f32),
            pltpu.VMEM((2, PAIR, W), f32),
            pltpu.VMEM((2, 2, PART, K), f32),
            pltpu.VMEM((2, PAIR, 2 * K), bf16),
            dma((ROWS // DCH,)), dma((8,)),
            dma((len(PIECES),)), dma((len(PIECES),)),
            dma((NZ - 1,)), dma((NZ - 1,)),
            dma((NZ, 3)), dma((NZ, 3)),
            dma((ng, 4)), dma((ng, 4)),
            dma((ng, 3)), dma((ng, 3)),
            dma((ng, 3)), dma((ng, 3)),
            dma((ng, 2)), dma((ng, 2)),
            dma((3, 2, NB)), dma((3, 2, NB)),
            dma((3,)), dma((3,)),
            dma((3,)), dma((3,)),
            dma((2,)), dma((2,)),
        ],
        compiler_params=pltpu.CompilerParams(
            collective_id=0, has_side_effects=True, vmem_limit_bytes=56 * 1024 * 1024),
    )(decoder_slab, encoder_panel)
    return out.reshape(ROWS, 1, W)


def solution(mesh):
    placed = (P("src", "hid"), P(("hid", "src"), "tgt"))
    return jax.shard_map(
        shards, mesh=mesh, in_specs=placed, out_specs=P("src", "tgt", "hid"), check_vma=False
    )
```
